32 devices in a mesh: groups: 2 (over x), node: 16 (over z, y, core).
Axes of the slice: x: 2, y: 2, z: 4, core: 2. Of those that a mesh axis runs over, the one named last changes fastest.
Arguments:
- mixer_input: bfloat16 [256, 4096], P(('groups', 'node')), parts along dimension 0, may hold values from -6 to 6
- chosen_experts: int32 [256, 8], P(('groups', 'node')), parts along dimension 0, may hold values from 0 to 7, as said below
- route_weight: float32 [256, 8], P(('groups', 'node')), parts along dimension 0, may hold values from 0.1 to 1
- gate_weight: bfloat16 [16, 4096, 384], P('node'), may hold values from -0.09375 to 0.09375
- up_weight: bfloat16 [16, 4096, 384], P('node'), may hold values from -0.09375 to 0.09375
- down_weight: bfloat16 [16, 384, 4096], P('node'), may hold values from -0.21875 to 0.21875
- queries: bfloat16 [128, 64, 128], P(('groups', 'node')), parts along dimension 0, may hold values from -6 to 6
- fresh_key: bfloat16 [128, 4, 128], P(('groups', 'node')), parts along dimension 0, may hold values from -15 to 15
- fresh_value: bfloat16 [128, 4, 128], P(('groups', 'node')), parts along dimension 0, may hold values from -6 to 6
- cache_key: bfloat16 [128, 4, 256, 128], P(('groups', 'node')), parts along dimension 0, may hold values from -64 to 64
- cache_value: bfloat16 [128, 4, 256, 128], P(('groups', 'node')), parts along dimension 0, may hold values from -6 to 6
- lengths: int32 [128], P(('groups', 'node')), parts along dimension 0, may hold values from 2 to 256, as said below
Outputs:
- expert_mix: bfloat16 [256, 4096], P(('groups', 'node')), parts along dimension 0
- attended: bfloat16 [128, 64, 128], P(('groups', 'node')), parts along dimension 0
The draws below stay inside these ranges and needn't reach their ends.
There are 2 independent parts, one for each index of `groups`. The reference program is written for one: setup_inputs(seed, part) draws one part's arguments, and reference() takes and returns one part's arrays. A program takes and returns all parts, laid end to end along the dimension named above; an argument that names none is the same for every part. Nothing has to cross between parts.
Inputs may be any that keep to these rules, and one draw needn't show every extreme that they name: `chosen_experts`: each row names 8 different experts; among the rows of one device no expert is named more than 8 times, and some expert is named exactly 8 times by the rows of every device. `lengths`: some sequence holds all 256 positions.
All inputs are finite; a program needn't handle non-finite values.
Results may differ from the reference program's by a relative error of at most 0.0058.
Values may be sent and summed in bfloat16 or wider, within the bound.
A program may use at most 64 MiB of HBM per device.

```python
import jax
import jax.numpy as jnp
from jax import lax

D = 4096
FF = 768
FH = 384
TOP = 8
Q_HEADS = 64
KV_HEADS = 4
HEAD_DIM = 128
GROUP = 16
TOK_DEV = 8
CTX = 256
EXPERTS = 8
CAP = 8
TOKENS = 128
SEQS = 64
N_NODE = 16


def draw_queries(key, part):
    key = jax.random.fold_in(key, 11)
    values = jnp.clip(jax.random.normal(key, (SEQS, Q_HEADS, HEAD_DIM), jnp.float32), -6.0, 6.0)
    return values.astype(jnp.bfloat16)


def draw_cache_key(key, part):
    key = jax.random.fold_in(key, 13)
    values = jnp.clip(jax.random.normal(key, (SEQS, KV_HEADS, CTX, HEAD_DIM), jnp.float32), -6.0, 6.0)
    return values.astype(jnp.bfloat16)


def draw_lengths(key, part):
    key = jax.random.fold_in(key, 7)
    first_key, second_key = jax.random.split(key)
    filled = jax.random.randint(first_key, (SEQS,), 2, CTX + 1)
    fullest = jax.random.randint(second_key, (), 0, SEQS)
    return filled.at[fullest].set(CTX).astype(jnp.int32)


def draw_chosen_experts(key, part):
    key = jax.random.fold_in(key, 5)
    busy_key, block_key = jax.random.split(key)
    busiest = jax.random.randint(busy_key, (), 0, EXPERTS)
    pick_total = CAP * (TOP - 1) + (TOK_DEV - CAP) * TOP
    distinct_need = TOP if TOK_DEV > CAP else TOP - 1
    least_period = max(distinct_need, -(-pick_total // CAP))

    def one_block(block_seed):
        order_key, period_key, shuffle_key, column_key = jax.random.split(block_seed, 4)
        ordering = jax.random.permutation(order_key, TOK_DEV)
        is_busy = jnp.zeros((TOK_DEV,), jnp.int32).at[ordering[:CAP]].set(1)
        counts = TOP - is_busy
        starts = jnp.cumsum(counts) - counts
        period_len = jax.random.randint(period_key, (), least_period, EXPERTS)
        shuffle = jax.random.permutation(shuffle_key, EXPERTS - 1)
        column = jnp.arange(TOP, dtype=jnp.int32)
        location = (starts[:, None] + column[None, :]) % period_len
        others = (busiest + 1 + shuffle[location]) % EXPERTS
        chosen = jnp.where(column[None, :] < counts[:, None], others, busiest)
        jitter_val = jax.random.randint(column_key, (TOK_DEV, TOP), 0, 1048576) * TOP + column[None, :]
        order_cols = jnp.argsort(jitter_val, axis=1)
        return jnp.take_along_axis(chosen, order_cols, axis=1)
    block_keys = jax.random.split(block_key, TOKENS // TOK_DEV)
    return jax.vmap(one_block)(block_keys).reshape(TOKENS, TOP).astype(jnp.int32)


def level_of(rng, extent, pieces, smallest, top_value):
    level = 1.0
    for position, shards_of in pieces:
        heights = jax.random.uniform(jax.random.fold_in(jax.random.fold_in(rng, 6), position), (shards_of,), jnp.float32, smallest / len(pieces), top_value / len(pieces))
        level = level * jnp.repeat(jnp.exp(heights), extent[position] // shards_of).reshape((-1,) + (1,) * (len(extent) - 1 - position))
    return level


def noise(rng, shape, width, limit, pieces=(), kind=jnp.bfloat16):
    factor_of = level_of(rng, shape, pieces, -0.22, 0.18) if pieces else 1.0
    values = jax.random.normal(rng, shape, jnp.float32) * width * factor_of
    return jnp.minimum(jnp.maximum(values, -limit), limit).astype(kind)


def setup_inputs(seed: int = 0, part: int = 0) -> dict:
    splits = jax.random.split(jax.random.key(seed), 13)
    own_keys = jax.random.split(jax.random.fold_in(splits[12], part), 13)
    return {
        "mixer_input": noise(own_keys[0], (TOKENS, D), 1.0, 6.0, ((0, 16),)),
        "chosen_experts": draw_chosen_experts(jax.random.fold_in(jax.random.fold_in(splits[12], part), 71), part),
        "route_weight": jnp.clip(0.1 + 0.9 * jax.random.uniform(own_keys[2], (TOKENS, TOP), jnp.float32) ** level_of(own_keys[2], (TOKENS, TOP), ((0, 16),), -0.2, 0.2), 0.1, 1.0),
        "gate_weight": noise(splits[3], (2 * EXPERTS, D, FH), D ** -0.5, 0.09375, ((0, 16),)),
        "up_weight": noise(splits[4], (2 * EXPERTS, D, FH), D ** -0.5, 0.09375, ((0, 16),)),
        "down_weight": noise(splits[5], (2 * EXPERTS, FH, D), FF ** -0.5, 0.21875, ((0, 16),)),
        "queries": draw_queries(jax.random.fold_in(jax.random.fold_in(splits[12], part), 71), part),
        "fresh_key": noise(own_keys[7], (SEQS, KV_HEADS, HEAD_DIM), 2.5, 15.0, ((0, 16),)),
        "fresh_value": noise(own_keys[8], (SEQS, KV_HEADS, HEAD_DIM), 1.0, 6.0, ((0, 16),)),
        "cache_key": draw_cache_key(jax.random.fold_in(jax.random.fold_in(splits[12], part), 71), part),
        "cache_value": noise(own_keys[10], (SEQS, KV_HEADS, CTX, HEAD_DIM), 1.0, 6.0, ((0, 16),)),
        "lengths": draw_lengths(jax.random.fold_in(jax.random.fold_in(splits[12], part), 71), part),
    }


def slot_numbers(chosen_experts):
    blocks = chosen_experts.reshape(N_NODE, TOK_DEV * TOP)
    onehot = (blocks[:, :, None] == jnp.arange(EXPERTS, dtype=jnp.int32)[None, None, :]).astype(jnp.int32)
    before = jnp.cumsum(onehot, axis=1) - onehot
    return jnp.sum(before * onehot, axis=2).reshape(TOKENS, TOP).astype(jnp.int32)


def mixture_layer(mixer_input, chosen_experts, route_weight, gate_weight, up_weight, down_weight):
    slot_rank = slot_numbers(chosen_experts)
    source = (jnp.arange(TOKENS, dtype=jnp.int32) // TOK_DEV)[:, None]
    target = (chosen_experts * (N_NODE * CAP) + source * CAP + slot_rank).astype(jnp.int32)
    token_index = jnp.repeat(jnp.arange(TOKENS, dtype=jnp.int32), TOP)
    owner_table = jnp.full((EXPERTS * N_NODE * CAP,), TOKENS, jnp.int32).at[target.reshape(-1)].set(token_index)
    owner_table = owner_table.reshape(EXPERTS, N_NODE * CAP)
    padded = jnp.concatenate([mixer_input, jnp.zeros((1, D), mixer_input.dtype)], axis=0)

    def run_expert(expert):
        row_block = jnp.take(padded, owner_table[expert], axis=0)
        partials = []
        for half_index in range(2):
            weight_row = 2 * expert + half_index
            gate_out = jnp.dot(row_block, gate_weight[weight_row], preferred_element_type=jnp.float32)
            up_out = jnp.dot(row_block, up_weight[weight_row], preferred_element_type=jnp.float32)
            hidden = (jax.nn.silu(gate_out) * up_out).astype(jnp.bfloat16)
            partials.append(jnp.dot(hidden, down_weight[weight_row], preferred_element_type=jnp.float32))
        return (partials[0] + partials[1]).astype(jnp.bfloat16)

    expert_out = lax.map(run_expert, jnp.arange(EXPERTS, dtype=jnp.int32))
    flat_rows = expert_out.reshape(EXPERTS * N_NODE * CAP, D)
    picked = jnp.take(flat_rows, target.reshape(-1), axis=0).reshape(TOKENS, TOP, D).astype(jnp.float32)
    share_norm = route_weight / jnp.sum(route_weight, axis=1, keepdims=True)
    return jnp.sum(share_norm[:, :, None] * picked, axis=1).astype(jnp.bfloat16)


def attend_sequence(packed):
    queries, fresh_key, fresh_value, cache_key, cache_value, length = packed
    grouped = queries.reshape(KV_HEADS, GROUP, HEAD_DIM).astype(jnp.float32)
    scaling = HEAD_DIM ** -0.5
    scores = jnp.einsum("kgd,kcd->kgc", grouped, cache_key.astype(jnp.float32)) * scaling
    own_score = jnp.einsum("kgd,kd->kg", grouped, fresh_key.astype(jnp.float32)) * scaling
    usable = jnp.arange(CTX, dtype=jnp.int32) < length
    masked = jnp.where(usable[None, None, :], scores, -jnp.inf)
    top_score = jnp.maximum(jnp.max(masked, axis=2), own_score)
    prob_rows = jnp.exp(masked - top_score[:, :, None])
    own_prob = jnp.exp(own_score - top_score)
    denominator = jnp.sum(prob_rows, axis=2) + own_prob
    prob_low = lax.optimization_barrier(prob_rows.astype(jnp.bfloat16)).astype(jnp.float32)
    own_low = lax.optimization_barrier(own_prob.astype(jnp.bfloat16)).astype(jnp.float32)
    numerator = jnp.einsum("kgc,kcd->kgd", prob_low, cache_value.astype(jnp.float32))
    numerator = numerator + own_low[:, :, None] * fresh_value.astype(jnp.float32)[:, None, :]
    return (numerator / denominator[:, :, None]).astype(jnp.bfloat16).reshape(Q_HEADS, HEAD_DIM)


def reference(mixer_input, chosen_experts, route_weight, gate_weight, up_weight, down_weight, queries, fresh_key, fresh_value, cache_key, cache_value, lengths):
    expert_mix = mixture_layer(mixer_input, chosen_experts, route_weight, gate_weight, up_weight, down_weight)
    attended = lax.map(attend_sequence, (queries, fresh_key, fresh_value, cache_key, cache_value, lengths))
    return (expert_mix, attended)
```

```python
import functools

import jax
import jax.numpy as jnp
from jax import lax
from jax.experimental import pallas as pl
from jax.experimental.pallas import tpu as pltpu
from jax.sharding import PartitionSpec as P

MESH = pl.DeviceIdType.MESH
F32 = jnp.float32
BF16 = jnp.bfloat16
PARTS = 4
LANES = 128
GROUP_BLOCKS = 16


def grid_of(node_count):
    chips = node_count // 2
    wide = 1
    while (2 * wide) * (2 * wide) <= chips and chips % (2 * wide) == 0:
        wide *= 2
    return chips // wide, wide


def kernel(
    tall, wide,
    x_ref, chosen_ref, route_ref, q_ref, fk_ref, fv_ref, len_ref,
    wg_hbm, wu_hbm, wd_hbm, ck_hbm, cv_hbm,
    mix_ref, att_ref,
    wg, wu, wd, ck, cv, gath, xs, hid, share,
    kept1, send1, recv1, kept2, send2, recv2, kept3, send3, recv3,
    load_sem, zs_sem, zr_sem, ys_sem, yr_sem, cs_sem, cr_sem,
    s1s, s1r, s2s, s2r, s3s, s3r,
):
    chips = tall * wide
    blocks = 2 * chips
    tokens, width = x_ref.shape
    half = width // 2
    part = half // PARTS
    me = lax.axis_index("node")
    core = me % 2
    y = (me // 2) % wide
    z = me // (2 * wide)

    def at_z(step):
        return {"node": ((z + step) % tall * wide + y) * 2 + core}

    def at_y(step):
        return {"node": (z * wide + (y + step) % wide) * 2 + core}

    partner = {"node": (z * wide + y) * 2 + 1 - core}

    loads = [
        pltpu.make_async_copy(src, dst, load_sem.at[i])
        for i, (src, dst) in enumerate(
            [(ck_hbm, ck), (cv_hbm, cv), (wg_hbm, wg), (wu_hbm, wu), (wd_hbm, wd)]
        )
    ]
    barrier = pltpu.get_barrier_semaphore()
    peers = [at_z(k) for k in range(1, tall)] + [at_y(j) for j in range(1, wide)] + [partner]
    for peer in peers:
        pl.semaphore_signal(barrier, inc=1, device_id=peer, device_id_type=MESH)
    for load in loads:
        load.start()

    route = route_ref[...]
    norm = route / jnp.sum(route, axis=1, keepdims=True)
    lane = lax.broadcasted_iota(jnp.int32, (tokens, LANES), 1)
    table = jnp.zeros((tokens, LANES), F32)
    chosen = chosen_ref[...]
    for k in range(chosen.shape[1]):
        table += jnp.where(lane == chosen[:, k : k + 1], norm[:, k : k + 1], 0.0)
    table_high = table.astype(BF16).astype(F32)
    xf = x_ref[...].astype(F32)
    gath[0, :, :half] = jnp.concatenate([xf[:, :half], xf[:, half:]], axis=0).astype(BF16)
    gath[0, :, half:] = jnp.concatenate([table_high, table - table_high], axis=0).astype(BF16)

    pl.semaphore_wait(barrier, len(peers))

    def block(dc, dy, dz):
        return (dc * wide + dy) * tall + dz

    sends = []

    def push(src, dst, ssem, rsem, device):
        copy = pltpu.make_async_remote_copy(
            src_ref=src, dst_ref=dst, send_sem=ssem, recv_sem=rsem,
            device_id=device, device_id_type=MESH,
        )
        copy.start()
        sends.append(copy)
        return copy

    z_copies = {}
    y_copies = {}
    c_copies = {}

    def to_y(dz):
        for j in range(1, wide):
            dy = wide - j
            i = dz * (wide - 1) + dy - 1
            y_copies[dy, dz] = push(
                gath.at[block(0, 0, dz)], gath.at[block(0, dy, dz)],
                ys_sem.at[i], yr_sem.at[i], at_y(j),
            )

    def to_core(dy, dz):
        i = dy * tall + dz
        c_copies[dy, dz] = push(
            gath.at[block(0, dy, dz)], gath.at[block(1, dy, dz)],
            cs_sem.at[i], cr_sem.at[i], partner,
        )

    to_y(0)
    for step in range(1, tall):
        k = (step + 1) // 2 if step % 2 else tall - step // 2
        dz = tall - k
        z_copies[dz] = push(
            gath.at[0], gath.at[dz], zs_sem.at[dz - 1], zr_sem.at[dz - 1], at_z(k)
        )
    to_core(0, 0)

    heads, head_width = ck.shape[1], ck.shape[3]
    context = ck.shape[2]
    seqs = ck.shape[0]
    group = q_ref.shape[1] // heads
    scaling = head_width ** (-0.5)

    def attend(s):
        queries = q_ref[s].reshape(heads, group, head_width)
        scores = (
            jnp.einsum("kgd,kcd->kgc", queries, ck[s], preferred_element_type=F32) * scaling
        )
        fk = fk_ref[s].astype(F32)
        own = (
            jnp.sum(queries.astype(F32) * fk[:, None, :], axis=2, keepdims=True) * scaling
        )
        column = lax.broadcasted_iota(jnp.int32, scores.shape, 2)
        masked = jnp.where(column < len_ref[s], scores, -jnp.inf)
        top = jnp.maximum(jnp.max(masked, axis=2, keepdims=True), own)
        prob = jnp.exp(masked - top)
        own_prob = jnp.exp(own - top)
        total = jnp.sum(prob, axis=2, keepdims=True) + own_prob
        mixed = jnp.einsum(
            "kgc,kcd->kgd", prob.astype(BF16), cv[s], preferred_element_type=F32
        )
        own_low = own_prob.astype(BF16).astype(F32)
        mixed = mixed + own_low * fv_ref[s].astype(F32)[:, None, :]
        att_ref[s] = (mixed / total).astype(BF16).reshape(heads * group, head_width)

    loads[0].wait()
    loads[1].wait()
    early = seqs // 2
    for s in range(early):
        attend(s)

    arrivals = []
    for step in range(1, tall):
        k = (step + 1) // 2 if step % 2 else tall - step // 2
        arrivals.append(tall - k)
    for dz in arrivals:
        z_copies[dz].wait_recv()
        to_y(dz)
        to_core(0, dz)
    for dz in [0] + arrivals:
        for dy in range(1, wide):
            y_copies[dy, dz].wait_recv()
            to_core(dy, dz)
    loads[2].wait()
    loads[3].wait()
    for dz in [0] + arrivals:
        for dy in range(wide):
            c_copies[dy, dz].wait_recv()

    per = min(blocks, GROUP_BLOCKS)
    rows = per * tokens
    expert = me // 2

    def first_half(start, at):
        for pair in range(per // 2):
            both = gath[pl.ds(start + 2 * pair, 2), :, :half].astype(F32)
            spot = pl.ds(pair * 2 * tokens, 2 * tokens)
            xs[spot, :half] = both[:, :tokens].reshape(2 * tokens, half).astype(BF16)
            xs[spot, half:] = both[:, tokens:].reshape(2 * tokens, half).astype(BF16)
        shares = gath[pl.ds(start, per), :, half:].astype(F32)
        shares = (shares[:, :tokens] + shares[:, tokens:]).reshape(rows, LANES)
        lanes = lax.broadcasted_iota(jnp.int32, (rows, LANES), 1)
        mine = jnp.sum(jnp.where(lanes == expert, shares, 0.0), axis=1, keepdims=True)
        share[pl.ds(at, rows), :] = jnp.broadcast_to(mine, (rows, LANES))
        gate = jnp.dot(xs[...], wg[0], preferred_element_type=F32)
        up = jnp.dot(xs[...], wu[0], preferred_element_type=F32)
        hid[pl.ds(at, rows), :] = (gate / (1.0 + jnp.exp(-gate)) * up).astype(BF16)

    groups = blocks // per
    if groups == 1:
        first_half(0, 0)
    else:

        @pl.loop(0, groups)
        def _(g):
            first_half(g * per, g * rows)

    loads[4].wait()

    def down(c, start, at):
        hidden = hid[pl.ds(at, rows), :]
        scale = share[pl.ds(at, rows), :1]
        sides = []
        for side in range(2):
            cols = pl.ds(side * half + c * part, part)
            out = jnp.dot(hidden, wd[0, :, cols], preferred_element_type=F32) * scale
            sides.append(out.reshape(per, tokens, part))
        return jnp.concatenate(sides, axis=1)

    def stage1(c):
        if groups == 1:
            out = down(c, 0, 0)
            send1[c] = out[chips:].astype(BF16)
            kept1[c] = out[:chips]
        else:

            @pl.loop(0, groups // 2)
            def _(g):
                send1[c, pl.ds(g * per, per)] = down(
                    c, chips + g * per, (groups // 2 + g) * rows
                ).astype(BF16)
                kept1[c, pl.ds(g * per, per)] = down(c, g * per, g * rows)

        return push(send1.at[c], recv1.at[c], s1s.at[c], s1r.at[c], partner)

    def stage2(c, before):
        before.wait_recv()
        copies = []
        for j in range(1, wide):
            span = pl.ds(j * tall, tall)
            send2[c, j - 1] = (kept1[c, span] + recv1[c, span].astype(F32)).astype(BF16)
            i = c * (wide - 1) + j - 1
            copies.append(
                push(send2.at[c, j - 1], recv2.at[c, j - 1], s2s.at[i], s2r.at[i], at_y(j))
            )
        span = pl.ds(0, tall)
        kept2[c] = kept1[c, span] + recv1[c, span].astype(F32)
        return copies

    def stage3(c, before):
        total = kept2[c]
        for j, copy in enumerate(before):
            copy.wait_recv()
            total = total + recv2[c, j].astype(F32)
        send3[c] = total[1:].astype(BF16)
        kept3[c] = total[0]
        copies = []
        for k in range(1, tall):
            i = c * (tall - 1) + k - 1
            copies.append(
                push(send3.at[c, k - 1], recv3.at[c, k - 1], s3s.at[i], s3r.at[i], at_z(k))
            )
        return copies

    def finish(c, before):
        total = kept3[c]
        for k, copy in enumerate(before):
            copy.wait_recv()
            total = total + recv3[c, k].astype(F32)
        mix_ref[:, pl.ds(c * part, part)] = total[:tokens].astype(BF16)
        mix_ref[:, pl.ds(half + c * part, part)] = total[tokens:].astype(BF16)

    ones, twos, threes = {}, {}, {}
    for c in range(PARTS):
        ones[c] = stage1(c)
        if c >= 1:
            twos[c - 1] = stage2(c - 1, ones[c - 1])
    twos[PARTS - 1] = stage2(PARTS - 1, ones[PARTS - 1])
    late = list(range(early, seqs))
    for c in range(PARTS):
        if late:
            attend(late.pop(0))
        threes[c] = stage3(c, twos[c])
    for s in late:
        attend(s)
    for c in range(PARTS):
        finish(c, threes[c])
    for copy in sends:
        copy.wait_send()


def body(
    mixer_input, chosen_experts, route_weight, gate_weight, up_weight, down_weight,
    queries, fresh_key, fresh_value, cache_key, cache_value, lengths,
):
    nodes = lax.axis_size("node")
    tall, wide = grid_of(nodes)
    chips = tall * wide
    tokens, width = mixer_input.shape
    hidden = gate_weight.shape[2]
    half = width // 2
    part = half // PARTS
    pair = 2 * tokens
    per = min(nodes, GROUP_BLOCKS)
    dma = pltpu.SemaphoreType.DMA
    vmem = pl.BlockSpec(memory_space=pltpu.VMEM)
    hbm = pl.BlockSpec(memory_space=pl.ANY)
    ys = max(1, wide - 1)
    zs = max(1, tall - 1)
    return pl.pallas_call(
        functools.partial(kernel, tall, wide),
        out_shape=(
            jax.ShapeDtypeStruct(mixer_input.shape, BF16),
            jax.ShapeDtypeStruct(queries.shape, BF16),
        ),
        in_specs=[vmem] * 6 + [pl.BlockSpec(memory_space=pltpu.SMEM)] + [hbm] * 5,
        out_specs=(vmem, vmem),
        scratch_shapes=[
            pltpu.VMEM(gate_weight.shape, BF16),
            pltpu.VMEM(up_weight.shape, BF16),
            pltpu.VMEM(down_weight.shape, BF16),
            pltpu.VMEM(cache_key.shape, BF16),
            pltpu.VMEM(cache_value.shape, BF16),
            pltpu.VMEM((nodes, pair, half + LANES), BF16),
            pltpu.VMEM((per * tokens, width), BF16),
            pltpu.VMEM((nodes * tokens, hidden), BF16),
            pltpu.VMEM((nodes * tokens, LANES), F32),
            pltpu.VMEM((PARTS, chips, pair, part), F32),
            pltpu.VMEM((PARTS, chips, pair, part), BF16),
            pltpu.VMEM((PARTS, chips, pair, part), BF16),
            pltpu.VMEM((PARTS, tall, pair, part), F32),
            pltpu.VMEM((PARTS, ys, tall, pair, part), BF16),
            pltpu.VMEM((PARTS, ys, tall, pair, part), BF16),
            pltpu.VMEM((PARTS, pair, part), F32),
            pltpu.VMEM((PARTS, zs, pair, part), BF16),
            pltpu.VMEM((PARTS, zs, pair, part), BF16),
            dma((5,)),
            dma((zs,)), dma((zs,)),
            dma((tall * ys,)), dma((tall * ys,)),
            dma((chips,)), dma((chips,)),
            dma((PARTS,)), dma((PARTS,)),
            dma((PARTS * ys,)), dma((PARTS * ys,)),
            dma((PARTS * zs,)), dma((PARTS * zs,)),
        ],
        compiler_params=pltpu.CompilerParams(
            collective_id=0, has_side_effects=True, vmem_limit_bytes=60 * 1024 * 1024
        ),
        name="moe_and_attention",
    )(
        mixer_input, chosen_experts, route_weight, queries, fresh_key, fresh_value, lengths,
        gate_weight, up_weight, down_weight, cache_key, cache_value,
    )


def solution(mesh):
    rows = P(("groups", "node"), None)
    node = P("node", None, None)
    seq3 = P(("groups", "node"), None, None)
    seq4 = P(("groups", "node"), None, None, None)
    in_specs = (
        rows, rows, rows, node, node, node,
        seq3, seq3, seq3, seq4, seq4, P(("groups", "node")),
    )
    return jax.shard_map(
        body, mesh=mesh, in_specs=in_specs, out_specs=(rows, seq3), check_vma=False
    )
```

```python
import functools

import jax
import jax.numpy as jnp
from jax import lax
from jax.experimental import pallas as pl
from jax.experimental.pallas import tpu as pltpu
from jax.sharding import PartitionSpec as P

MESH = pl.DeviceIdType.MESH
F32 = jnp.float32
BF16 = jnp.bfloat16
PARTS = 4
LANES = 128
GROUP_BLOCKS = 16


def grid_of(node_count):
    chips = node_count // 2
    wide = 1
    while (2 * wide) * (2 * wide) <= chips and chips % (2 * wide) == 0:
        wide *= 2
    return chips // wide, wide


def kernel(
    tall, wide,
    x_ref, chosen_ref, route_ref, q_ref, fk_ref, fv_ref, len_ref,
    wg_hbm, wu_hbm, wd_hbm, ck_hbm, cv_hbm,
    mix_ref, att_ref,
    wg, wu, wd, ck, cv, gath, xs, hid, share,
    kept1, send1, recv1, kept2, send2, recv2, kept3, send3, recv3,
    load_sem, zs_sem, zr_sem, ys_sem, yr_sem, cs_sem, cr_sem,
    s1s, s1r, s2s, s2r, s3s, s3r,
):
    chips = tall * wide
    blocks = 2 * chips
    tokens, width = x_ref.shape
    half = width // 2
    part = half // PARTS
    me = lax.axis_index("node")
    core = me % 2
    y = (me // 2) % wide
    z = me // (2 * wide)

    def at_z(step):
        return {"node": ((z + step) % tall * wide + y) * 2 + core}

    def at_y(step):
        return {"node": (z * wide + (y + step) % wide) * 2 + core}

    partner = {"node": (z * wide + y) * 2 + 1 - core}

    loads = [
        pltpu.make_async_copy(src, dst, load_sem.at[i])
        for i, (src, dst) in enumerate(
            [(ck_hbm, ck), (cv_hbm, cv), (wg_hbm, wg), (wu_hbm, wu), (wd_hbm, wd)]
        )
    ]
    barrier = pltpu.get_barrier_semaphore()
    peers = [at_z(k) for k in range(1, tall)] + [at_y(j) for j in range(1, wide)] + [partner]
    for peer in peers:
        pl.semaphore_signal(barrier, inc=1, device_id=peer, device_id_type=MESH)
    for load in loads:
        load.start()

    route = route_ref[...]
    norm = route / jnp.sum(route, axis=1, keepdims=True)
    lane = lax.broadcasted_iota(jnp.int32, (tokens, LANES), 1)
    table = jnp.zeros((tokens, LANES), F32)
    chosen = chosen_ref[...]
    for k in range(chosen.shape[1]):
        table += jnp.where(lane == chosen[:, k : k + 1], norm[:, k : k + 1], 0.0)
    table_high = table.astype(BF16).astype(F32)
    xf = x_ref[...].astype(F32)
    gath[0, :, :half] = jnp.concatenate([xf[:, :half], xf[:, half:]], axis=0).astype(BF16)
    gath[0, :, half:] = jnp.concatenate([table_high, table - table_high], axis=0).astype(BF16)

    pl.semaphore_wait(barrier, len(peers))

    def block(dc, dy, dz):
        return (dc * wide + dy) * tall + dz

    sends = []

    def push(src, dst, ssem, rsem, device):
        copy = pltpu.make_async_remote_copy(
            src_ref=src, dst_ref=dst, send_sem=ssem, recv_sem=rsem,
            device_id=device, device_id_type=MESH,
        )
        copy.start()
        sends.append(copy)
        return copy

    z_copies = {}
    y_copies = {}
    c_copies = {}

    def to_y(dz):
        for j in range(1, wide):
            dy = wide - j
            i = dz * (wide - 1) + dy - 1
            y_copies[dy, dz] = push(
                gath.at[block(0, 0, dz)], gath.at[block(0, dy, dz)],
                ys_sem.at[i], yr_sem.at[i], at_y(j),
            )

    def to_core(dy, dz):
        i = dy * tall + dz
        c_copies[dy, dz] = push(
            gath.at[block(0, dy, dz)], gath.at[block(1, dy, dz)],
            cs_sem.at[i], cr_sem.at[i], partner,
        )

    to_y(0)
    for step in range(1, tall):
        k = (step + 1) // 2 if step % 2 else tall - step // 2
        dz = tall - k
        z_copies[dz] = push(
            gath.at[0], gath.at[dz], zs_sem.at[dz - 1], zr_sem.at[dz - 1], at_z(k)
        )
    to_core(0, 0)

    heads, head_width = ck.shape[1], ck.shape[3]
    context = ck.shape[2]
    seqs = ck.shape[0]
    group = q_ref.shape[1] // heads
    scaling = head_width ** (-0.5)

    def attend(s):
        queries = q_ref[s].reshape(heads, group, head_width)
        scores = (
            jnp.einsum("kgd,kcd->kgc", queries, ck[s], preferred_element_type=F32) * scaling
        )
        fk = fk_ref[s].astype(F32)
        own = (
            jnp.sum(queries.astype(F32) * fk[:, None, :], axis=2, keepdims=True) * scaling
        )
        column = lax.broadcasted_iota(jnp.int32, scores.shape, 2)
        masked = jnp.where(column < len_ref[s], scores, -jnp.inf)
        top = jnp.maximum(jnp.max(masked, axis=2, keepdims=True), own)
        prob = jnp.exp(masked - top)
        own_prob = jnp.exp(own - top)
        total = jnp.sum(prob, axis=2, keepdims=True) + own_prob
        mixed = jnp.einsum(
            "kgc,kcd->kgd", prob.astype(BF16), cv[s], preferred_element_type=F32
        )
        own_low = own_prob.astype(BF16).astype(F32)
        mixed = mixed + own_low * fv_ref[s].astype(F32)[:, None, :]
        att_ref[s] = (mixed / total).astype(BF16).reshape(heads * group, head_width)

    loads[0].wait()
    loads[1].wait()
    early = seqs // 2
    for s in range(early):
        attend(s)

    arrivals = []
    for step in range(1, tall):
        k = (step + 1) // 2 if step % 2 else tall - step // 2
        arrivals.append(tall - k)
    for dz in arrivals:
        z_copies[dz].wait_recv()
        to_y(dz)
        to_core(0, dz)
    for dz in [0] + arrivals:
        for dy in range(1, wide):
            y_copies[dy, dz].wait_recv()
            to_core(dy, dz)
    loads[2].wait()
    loads[3].wait()
    for dz in [0] + arrivals:
        for dy in range(wide):
            c_copies[dy, dz].wait_recv()

    per = min(blocks, GROUP_BLOCKS)
    rows = per * tokens
    expert = me // 2

    def first_half(start, at):
        for pair in range(per // 2):
            both = gath[pl.ds(start + 2 * pair, 2), :, :half].astype(F32)
            spot = pl.ds(pair * 2 * tokens, 2 * tokens)
            xs[spot, :half] = both[:, :tokens].reshape(2 * tokens, half).astype(BF16)
            xs[spot, half:] = both[:, tokens:].reshape(2 * tokens, half).astype(BF16)
        shares = gath[pl.ds(start, per), :, half:].astype(F32)
        shares = (shares[:, :tokens] + shares[:, tokens:]).reshape(rows, LANES)
        lanes = lax.broadcasted_iota(jnp.int32, (rows, LANES), 1)
        mine = jnp.sum(jnp.where(lanes == expert, shares, 0.0), axis=1, keepdims=True)
        share[pl.ds(at, rows), :] = jnp.broadcast_to(mine, (rows, LANES))
        gate = jnp.dot(xs[...], wg[0], preferred_element_type=F32)
        up = jnp.dot(xs[...], wu[0], preferred_element_type=F32)
        hid[pl.ds(at, rows), :] = (gate / (1.0 + jnp.exp(-gate)) * up).astype(BF16)

    groups = blocks // per
    if groups == 1:
        first_half(0, 0)
    else:

        @pl.loop(0, groups)
        def _(g):
            first_half(g * per, g * rows)

    loads[4].wait()

    def down(c, start, at):
        hidden = hid[pl.ds(at, rows), :]
        scale = share[pl.ds(at, rows), :1]
        sides = []
        for side in range(2):
            cols = pl.ds(side * half + c * part, part)
            out = jnp.dot(hidden, wd[0, :, cols], preferred_element_type=F32) * scale
            sides.append(out.reshape(per, tokens, part))
        return jnp.concatenate(sides, axis=1)

    def stage1(c):
        if groups == 1:
            out = down(c, 0, 0)
            send1[c] = out[chips:].astype(BF16)
            kept1[c] = out[:chips]
        else:

            @pl.loop(0, groups // 2)
            def _(g):
                send1[c, pl.ds(g * per, per)] = down(
                    c, chips + g * per, (groups // 2 + g) * rows
                ).astype(BF16)
                kept1[c, pl.ds(g * per, per)] = down(c, g * per, g * rows)

        return push(send1.at[c], recv1.at[c], s1s.at[c], s1r.at[c], partner)

    def stage2(c, before):
        before.wait_recv()
        copies = []
        for j in range(1, wide):
            span = pl.ds(j * tall, tall)
            send2[c, j - 1] = (kept1[c, span] + recv1[c, span].astype(F32)).astype(BF16)
            i = c * (wide - 1) + j - 1
            copies.append(
                push(send2.at[c, j - 1], recv2.at[c, j - 1], s2s.at[i], s2r.at[i], at_y(j))
            )
        span = pl.ds(0, tall)
        kept2[c] = kept1[c, span] + recv1[c, span].astype(F32)
        return copies

    def stage3(c, before):
        total = kept2[c]
        for j, copy in enumerate(before):
            copy.wait_recv()
            total = total + recv2[c, j].astype(F32)
        send3[c] = total[1:].astype(BF16)
        kept3[c] = total[0]
        copies = []
        for k in range(1, tall):
            i = c * (tall - 1) + k - 1
            copies.append(
                push(send3.at[c, k - 1], recv3.at[c, k - 1], s3s.at[i], s3r.at[i], at_z(k))
            )
        return copies

    def finish(c, before):
        total = kept3[c]
        for k, copy in enumerate(before):
            copy.wait_recv()
            total = total + recv3[c, k].astype(F32)
        mix_ref[:, pl.ds(c * part, part)] = total[:tokens].astype(BF16)
        mix_ref[:, pl.ds(half + c * part, part)] = total[tokens:].astype(BF16)

    ones, twos, threes = {}, {}, {}
    for c in range(PARTS):
        ones[c] = stage1(c)
        if c >= 1:
            twos[c - 1] = stage2(c - 1, ones[c - 1])
    twos[PARTS - 1] = stage2(PARTS - 1, ones[PARTS - 1])
    late = list(range(early, seqs))
    for c in range(PARTS):
        if late:
            attend(late.pop(0))
        threes[c] = stage3(c, twos[c])
    for s in late:
        attend(s)
    for c in range(PARTS):
        finish(c, threes[c])
    for copy in sends:
        copy.wait_send()


def place(mix_in, att_in, mix_out, att_out):
    mix_out[...] = mix_in[...]
    att_out[...] = att_in[...]


def body(
    mixer_input, chosen_experts, route_weight, gate_weight, up_weight, down_weight,
    queries, fresh_key, fresh_value, cache_key, cache_value, lengths,
):
    nodes = lax.axis_size("node")
    tall, wide = grid_of(nodes)
    chips = tall * wide
    tokens, width = mixer_input.shape
    hidden = gate_weight.shape[2]
    half = width // 2
    part = half // PARTS
    pair = 2 * tokens
    per = min(nodes, GROUP_BLOCKS)
    dma = pltpu.SemaphoreType.DMA
    vmem = pl.BlockSpec(memory_space=pltpu.VMEM)
    hbm = pl.BlockSpec(memory_space=pl.ANY)
    ys = max(1, wide - 1)
    zs = max(1, tall - 1)
    mixture, attended = pl.pallas_call(
        functools.partial(kernel, tall, wide),
        out_shape=(
            jax.ShapeDtypeStruct(mixer_input.shape, BF16),
            jax.ShapeDtypeStruct(queries.shape, BF16),
        ),
        in_specs=[vmem] * 6 + [pl.BlockSpec(memory_space=pltpu.SMEM)] + [hbm] * 5,
        out_specs=(vmem, vmem),
        scratch_shapes=[
            pltpu.VMEM(gate_weight.shape, BF16),
            pltpu.VMEM(up_weight.shape, BF16),
            pltpu.VMEM(down_weight.shape, BF16),
            pltpu.VMEM(cache_key.shape, BF16),
            pltpu.VMEM(cache_value.shape, BF16),
            pltpu.VMEM((nodes, pair, half + LANES), BF16),
            pltpu.VMEM((per * tokens, width), BF16),
            pltpu.VMEM((nodes * tokens, hidden), BF16),
            pltpu.VMEM((nodes * tokens, LANES), F32),
            pltpu.VMEM((PARTS, chips, pair, part), F32),
            pltpu.VMEM((PARTS, chips, pair, part), BF16),
            pltpu.VMEM((PARTS, chips, pair, part), BF16),
            pltpu.VMEM((PARTS, tall, pair, part), F32),
            pltpu.VMEM((PARTS, ys, tall, pair, part), BF16),
            pltpu.VMEM((PARTS, ys, tall, pair, part), BF16),
            pltpu.VMEM((PARTS, pair, part), F32),
            pltpu.VMEM((PARTS, zs, pair, part), BF16),
            pltpu.VMEM((PARTS, zs, pair, part), BF16),
            dma((5,)),
            dma((zs,)), dma((zs,)),
            dma((tall * ys,)), dma((tall * ys,)),
            dma((chips,)), dma((chips,)),
            dma((PARTS,)), dma((PARTS,)),
            dma((PARTS * ys,)), dma((PARTS * ys,)),
            dma((PARTS * zs,)), dma((PARTS * zs,)),
        ],
        compiler_params=pltpu.CompilerParams(
            collective_id=0, has_side_effects=True, vmem_limit_bytes=60 * 1024 * 1024
        ),
        name="moe_and_attention",
    )(
        mixer_input, chosen_experts, route_weight, queries, fresh_key, fresh_value, lengths,
        gate_weight, up_weight, down_weight, cache_key, cache_value,
    )
    return pl.pallas_call(
        place,
        out_shape=(
            jax.ShapeDtypeStruct(mixture.shape, BF16),
            jax.ShapeDtypeStruct(attended.shape, BF16),
        ),
        in_specs=[vmem] * 2,
        out_specs=(vmem, vmem),
        name="place_results",
    )(mixture, attended)


def solution(mesh):
    rows = P(("groups", "node"), None)
    node = P("node", None, None)
    seq3 = P(("groups", "node"), None, None)
    seq4 = P(("groups", "node"), None, None, None)
    in_specs = (
        rows, rows, rows, node, node, node,
        seq3, seq3, seq3, seq4, seq4, P(("groups", "node")),
    )
    return jax.shard_map(
        body, mesh=mesh, in_specs=in_specs, out_specs=(rows, seq3), check_vma=False
    )
```
